32 devices in a mesh: src: 2 (over y), tp: 8 (over z, x), row: 2 (over core).
Axes of the slice: x: 2, y: 2, z: 4, core: 2. Of those that a mesh axis runs over, the one named last changes fastest.
Arguments:
- tokens: bfloat16 [2, 256, 8192], P('src', 'tp', 'row'), may hold values from -6 to 6
- coefficients: float32 [2, 2], replicated, may hold values from -2 to 2
- gate_weights: bfloat16 [2, 8192, 4096], P('src', 'row', 'tp'), may hold values from -0.0625 to 0.0625
- up_weights: bfloat16 [2, 8192, 4096], P('src', 'row', 'tp'), may hold values from -0.0625 to 0.0625
Outputs:
- hidden: bfloat16 [2, 256, 4096], P('src', 'row', 'tp')
The draws below stay inside these ranges and needn't reach their ends.
All inputs are finite; a program needn't handle non-finite values.
Results may differ from the reference program's by a relative error of at most 0.0013.
Values may be sent and summed in bfloat16 or wider, within the bound.
No kernel may reach another device: no remote copies, remote signals or barrier semaphores. Data moves between devices by JAX's collectives and lax.ppermute only.
A program may use at most 64 MiB of HBM per device.

```python
import jax
import jax.numpy as jnp
from jax import lax

D = 8192
FF = 4096
TOK = 256
K = 2
M = 2


def block_levels(key, shape, cuts, low, top_value):
    gain, own = 1.0, jax.random.fold_in(key, 6)
    for dim, blocks in cuts:
        steps = jnp.exp(jax.random.uniform(jax.random.fold_in(own, dim), (blocks,), jnp.float32, low / len(cuts), top_value / len(cuts)))
        gain = gain * jnp.repeat(steps, shape[dim] // blocks).reshape([-1 if axis == dim else 1 for axis in range(len(shape))])
    return gain


def noise(key, extent, width, bound, cuts=(), kind=jnp.bfloat16):
    drawn = width * jax.random.normal(key, extent, jnp.float32)
    if cuts:
        drawn = drawn * block_levels(key, extent, cuts, -0.22, 0.18)
    return jnp.clip(drawn, -bound, bound).astype(kind)


def setup_inputs(seed: int = 0) -> dict:
    splits = jax.random.split(jax.random.key(seed), 5)
    tokens = noise(splits[0], (M, TOK, D), 1.0, 6.0, ((0, 2), (1, 8), (2, 2)))
    coefficients = noise(splits[1], (M, K), 0.35, 2.0, (), jnp.float32)
    gate_weights = noise(splits[2], (K, D, FF), D ** -0.5, 0.0625, ((0, 2), (1, 2), (2, 8)))
    up_weights = noise(splits[3], (K, D, FF), D ** -0.5, 0.0625, ((0, 2), (1, 2), (2, 8)))
    return {"tokens": tokens, "coefficients": coefficients, "gate_weights": gate_weights, "up_weights": up_weights}


def reference(tokens, coefficients, gate_weights, up_weights):
    def one_candidate(candidate):
        row_weights = coefficients[candidate]

        def add_source(source, totals):
            merged_gate, merged_up = totals
            gate_slab = lax.dynamic_index_in_dim(gate_weights, source, 0, keepdims=False).astype(jnp.float32)
            up_slab = lax.dynamic_index_in_dim(up_weights, source, 0, keepdims=False).astype(jnp.float32)
            factor = row_weights[source]
            return (merged_gate + factor * gate_slab, merged_up + factor * up_slab)

        zeros_start = jnp.zeros((D, FF), jnp.float32)
        merged_gate, merged_up = lax.fori_loop(0, K, add_source, (zeros_start, zeros_start))
        inputs = tokens[candidate].astype(jnp.float32)
        gate = jnp.dot(inputs, merged_gate, precision=lax.Precision.HIGHEST, preferred_element_type=jnp.float32)
        upper = jnp.dot(inputs, merged_up, precision=lax.Precision.HIGHEST, preferred_element_type=jnp.float32)
        return (jax.nn.silu(gate) * upper).astype(jnp.bfloat16)

    return lax.map(one_candidate, jnp.arange(M))
```

```python
import jax
import jax.numpy as jnp
from jax import lax
from jax.experimental import pallas as pl
from jax.experimental.pallas import tpu as pltpu
from jax.sharding import PartitionSpec as P

AXES = ("src", "tp", "row")


def gathered(tokens, coefficients, gate_weights, up_weights):
    local_rows = tokens.shape[1]
    half_width = tokens.shape[2]
    candidates = coefficients.shape[0]
    sources = coefficients.shape[1]
    per_candidate = local_rows * lax.axis_size("tp")
    out_rows = per_candidate // lax.axis_size("row")
    own_source = lax.axis_index("src")
    picked = (jnp.arange(sources, dtype=jnp.int32) == own_source).astype(jnp.float32)
    own_factors = jnp.sum(coefficients * picked[None, :], axis=1)
    gate_local = gate_weights[0]
    up_local = up_weights[0]
    hidden_width = gate_local.shape[1]
    flat_tokens = tokens.reshape(local_rows, half_width)
    row_block = lax.all_gather(flat_tokens, ("src", "tp"), axis=0, tiled=True)
    owner_ids = jnp.arange(row_block.shape[0], dtype=jnp.int32) // per_candidate
    one_hot = (owner_ids[:, None] == jnp.arange(candidates, dtype=jnp.int32)[None, :]).astype(
        jnp.float32
    )
    factor = jnp.sum(one_hot * own_factors[None, :], axis=1)[:, None]
    gate_part = jnp.dot(row_block, gate_local, preferred_element_type=jnp.float32)
    up_part = jnp.dot(row_block, up_local, preferred_element_type=jnp.float32)
    collected = jnp.concatenate((gate_part, up_part), axis=1) * factor
    summed = lax.psum_scatter(collected, ("src", "row"), scatter_dimension=0, tiled=True)
    hidden = (jax.nn.silu(summed[:, :hidden_width]) * summed[:, hidden_width:]).astype(jnp.bfloat16)
    return hidden.reshape(1, out_rows, hidden_width)


def products(blocks, factors, gate_weights, up_weights):
    count = len(blocks)
    rows, depth = blocks[0].shape
    width = gate_weights.shape[2]
    step = min(depth, 1024)

    def kernel(*refs):
        scale, block_refs = refs[0], refs[1 : count + 1]
        gate, up, out = refs[count + 1 :]
        lhs = jnp.concatenate([ref[...] for ref in block_refs], axis=0)
        first = pl.program_id(0) == 0
        last = pl.program_id(0) == pl.num_programs(0) - 1
        for start, weights in ((0, gate), (width, up)):
            part = jnp.dot(lhs, weights[0], preferred_element_type=jnp.float32)
            columns = slice(start, start + width)

            @pl.when(first)
            def _():
                out[:, columns] = part

            @pl.when(jnp.logical_not(first))
            def _():
                out[:, columns] += part

        @pl.when(last)
        def _():
            for i in range(count):
                span = slice(i * rows, (i + 1) * rows)
                out[span, :] = out[span, :] * scale[i]

    return pl.pallas_call(
        kernel,
        grid=(depth // step,),
        out_shape=jax.ShapeDtypeStruct((count * rows, 2 * width), jnp.float32),
        in_specs=[pl.BlockSpec(memory_space=pltpu.SMEM)]
        + [pl.BlockSpec((rows, step), lambda k: (0, k))] * count
        + [pl.BlockSpec((1, step, width), lambda k: (0, k, 0))] * 2,
        out_specs=pl.BlockSpec((count * rows, 2 * width), lambda k: (0, 0)),
        compiler_params=pltpu.CompilerParams(vmem_limit_bytes=24 * 2**20),
        cost_estimate=pl.CostEstimate(
            flops=4 * count * rows * depth * width,
            bytes_accessed=4 * depth * width + 2 * count * rows * depth,
            transcendentals=0,
        ),
    )(jnp.stack(factors), *blocks, gate_weights, up_weights)


def paired(mesh):
    tp = mesh.shape["tp"]
    levels = tp // 2
    half = levels // 2

    def place(src, z, x, row):
        return (src * tp + z * 2 + x) * 2 + row

    every = [(s, z, x, r) for s in range(2) for z in range(levels) for x in range(2) for r in range(2)]

    def swap(array, src=0, z=0, x=0):
        pairs = [(place(*at), place(at[0] ^ src, at[1] ^ z, at[2] ^ x, at[3])) for at in every]
        return lax.ppermute(array, AXES, pairs)

    def to_owner(array, far):
        pairs = [
            (place(s, z, x, r), place(s, z, x, r ^ 1)) for s, z, x, r in every if (r == z // half) == far
        ]
        return lax.ppermute(array, AXES, pairs)

    def owner_src(array, far):
        pairs = [
            (place(s, z, x, r), place(s ^ 1, z, x, r)) for s, z, x, r in every if (r == z // half) != far
        ]
        return lax.ppermute(array, AXES, pairs)

    def shards(tokens, coefficients, gate_weights, up_weights):
        rows = tokens.shape[1]
        own_src, own_tp, own_row = (lax.axis_index(name) for name in AXES)
        picked = jnp.where(own_src == 0, coefficients[:, 0], coefficients[:, 1])
        own_factor = jnp.where(own_src == 0, picked[0], picked[1])
        other_factor = jnp.where(own_src == 0, picked[1], picked[0])

        b0 = tokens[0]
        z1 = swap(b0, z=1)
        x0 = swap(b0, x=1)
        y0 = swap(b0, src=1)
        z2 = swap(b0, z=2)
        z3 = swap(b0, z=3)
        y1, x1 = swap(z1, src=1), swap(z1, x=1)
        d0 = swap(y0, x=1)
        d1 = swap(d0, z=1)
        y2, x2 = swap(z2, src=1), swap(z2, x=1)
        d2 = swap(d0, z=2)
        y3, x3 = swap(z3, src=1), swap(z3, x=1)
        d3 = swap(d2, z=1)

        own4 = [own_factor] * 4
        other4 = [other_factor] * 4
        near = products(
            [y0, d0, y1, d1, b0, x0, z1, x1], other4 + own4, gate_weights, up_weights
        )
        near = near + to_owner(near, False)
        split = 4 * rows
        near_other = owner_src(near[:split], False)
        far_other = products([y2, d2, y3, d3], other4, gate_weights, up_weights)
        far_other = far_other + to_owner(far_other, True)
        far_other = owner_src(far_other, True)
        far_own = products([z2, x2, z3, x3], own4, gate_weights, up_weights)
        far_sum = far_own + to_owner(far_own, True) + far_other
        near_sum = near[split:] + near_other

        keeps_near = own_row == own_tp // 2 // half
        total = jnp.where(keeps_near, near_sum, far_sum)
        width = gate_weights.shape[2]
        hidden = (jax.nn.silu(total[:, :width]) * total[:, width:]).astype(jnp.bfloat16)
        hidden = hidden.reshape(2, 2, rows, width)
        hidden = jnp.where(own_tp % 2 == 0, hidden, hidden[:, ::-1])
        hidden = jnp.where(own_tp // 2 % 2 == 0, hidden, hidden[::-1])
        return hidden.reshape(1, 4 * rows, width)

    return shards


def solution(mesh):
    fits = mesh.shape["src"] == 2 and mesh.shape["tp"] == 8 and mesh.shape["row"] == 2
    return jax.shard_map(
        paired(mesh) if fits else gathered,
        mesh=mesh,
        in_specs=(P("src", "tp", "row"), P(), P("src", "row", "tp"), P("src", "row", "tp")),
        out_specs=P("src", "row", "tp"),
        check_vma=False,
    )
```

```python
import jax
import jax.numpy as jnp
from jax import lax
from jax.experimental import pallas as pl
from jax.experimental.pallas import tpu as pltpu
from jax.sharding import PartitionSpec as P

AXES = ("src", "tp", "row")


def gathered(tokens, coefficients, gate_weights, up_weights):
    local_rows = tokens.shape[1]
    half_width = tokens.shape[2]
    candidates = coefficients.shape[0]
    sources = coefficients.shape[1]
    per_candidate = local_rows * lax.axis_size("tp")
    out_rows = per_candidate // lax.axis_size("row")
    own_source = lax.axis_index("src")
    picked = (jnp.arange(sources, dtype=jnp.int32) == own_source).astype(jnp.float32)
    own_factors = jnp.sum(coefficients * picked[None, :], axis=1)
    gate_local = gate_weights[0]
    up_local = up_weights[0]
    hidden_width = gate_local.shape[1]
    flat_tokens = tokens.reshape(local_rows, half_width)
    row_block = lax.all_gather(flat_tokens, ("src", "tp"), axis=0, tiled=True)
    owner_ids = jnp.arange(row_block.shape[0], dtype=jnp.int32) // per_candidate
    one_hot = (owner_ids[:, None] == jnp.arange(candidates, dtype=jnp.int32)[None, :]).astype(
        jnp.float32
    )
    factor = jnp.sum(one_hot * own_factors[None, :], axis=1)[:, None]
    gate_part = jnp.dot(row_block, gate_local, preferred_element_type=jnp.float32)
    up_part = jnp.dot(row_block, up_local, preferred_element_type=jnp.float32)
    collected = jnp.concatenate((gate_part, up_part), axis=1) * factor
    summed = lax.psum_scatter(collected, ("src", "row"), scatter_dimension=0, tiled=True)
    hidden = (jax.nn.silu(summed[:, :hidden_width]) * summed[:, hidden_width:]).astype(jnp.bfloat16)
    return hidden.reshape(1, out_rows, hidden_width)


def after(array, *others):
    return lax.optimization_barrier((array,) + others)[0]


def products(blocks, scales, coefficients, gate_weights, up_weights, work=1):
    count = len(blocks)
    rows, depth = blocks[0].shape
    width = gate_weights.shape[2]

    def kernel(*refs):
        table, block_refs = refs[0], refs[1 : count + 1]
        gate, up, out = refs[count + 1 :]
        source = lax.axis_index("src")
        factors = (table[source, source], table[1 - source, source])
        lhs = jnp.concatenate([ref[...] for ref in block_refs], axis=0)
        for start, weights in ((0, gate), (width, up)):
            part = jnp.dot(lhs, weights[0], preferred_element_type=jnp.float32)
            for i in range(count):
                span = slice(i * rows, (i + 1) * rows)
                out[span, start : start + width] = part[span] * factors[scales[i]]

    whole = pl.BlockSpec(memory_space=pltpu.VMEM)
    return pl.pallas_call(
        kernel,
        out_shape=jax.ShapeDtypeStruct((count * rows, 2 * width), jnp.float32),
        in_specs=[pl.BlockSpec(memory_space=pltpu.SMEM)] + [whole] * (count + 2),
        out_specs=whole,
        compiler_params=pltpu.CompilerParams(vmem_limit_bytes=24 * 2**20),
        cost_estimate=pl.CostEstimate(
            flops=work * 4 * count * rows * depth * width,
            bytes_accessed=4 * depth * width + 2 * count * rows * depth,
            transcendentals=0,
        ),
    )(coefficients, *blocks, gate_weights, up_weights)


def resident(gate_weights, up_weights, work):
    def kernel(gate, up, gate_out, up_out, sems):
        copies = [
            pltpu.make_async_copy(gate, gate_out, sems.at[0]),
            pltpu.make_async_copy(up, up_out, sems.at[1]),
        ]
        for copy in copies:
            copy.start()
        for copy in copies:
            copy.wait()

    size = gate_weights.size + up_weights.size
    return pl.pallas_call(
        kernel,
        out_shape=[pltpu.VMEM(w.shape, w.dtype) for w in (gate_weights, up_weights)],
        in_specs=[pl.BlockSpec(memory_space=pltpu.HBM)] * 2,
        out_specs=[pl.BlockSpec(memory_space=pltpu.VMEM)] * 2,
        scratch_shapes=[pltpu.SemaphoreType.DMA((2,))],
        compiler_params=pltpu.CompilerParams(vmem_limit_bytes=48 * 2**20),
        cost_estimate=pl.CostEstimate(
            flops=work * size, bytes_accessed=4 * size, transcendentals=0
        ),
    )(gate_weights, up_weights)


def activated(total_parts, keeps_near, swap_x, swap_z, rows, width):
    def kernel(flags, *refs):
        out = refs[-1]
        near, far = refs[:3], refs[3:6]

        def write(parts):
            for i in range(4):
                span = slice(i * rows, (i + 1) * rows)
                total = parts[0][span, :] + parts[1][span, :] + parts[2][span, :]
                gate, up = total[:, :width], total[:, width:]
                value = (gate / (1 + jnp.exp(-gate)) * up).astype(jnp.bfloat16)
                at = (i & 1) ^ flags[1] | (((i >> 1) ^ flags[2]) << 1)
                out[0, pl.ds(pl.multiple_of(at * rows, rows), rows), :] = value

        @pl.when(flags[0] == 1)
        def _():
            write(near)

        @pl.when(flags[0] == 0)
        def _():
            write(far)

    whole = pl.BlockSpec(memory_space=pltpu.VMEM)
    flags = jnp.stack([keeps_near, swap_x, swap_z]).astype(jnp.int32)
    return pl.pallas_call(
        kernel,
        out_shape=jax.ShapeDtypeStruct((1, 4 * rows, width), jnp.bfloat16),
        in_specs=[pl.BlockSpec(memory_space=pltpu.SMEM)] + [whole] * 6,
        out_specs=whole,
        compiler_params=pltpu.CompilerParams(vmem_limit_bytes=24 * 2**20),
    )(flags, *total_parts)


def paired(mesh):
    tp = mesh.shape["tp"]
    levels = tp // 2
    half = levels // 2

    def place(src, z, x, row):
        return (src * tp + z * 2 + x) * 2 + row

    every = [(s, z, x, r) for s in range(2) for z in range(levels) for x in range(2) for r in range(2)]

    def swap(array, src=0, z=0, x=0):
        pairs = [(place(*at), place(at[0] ^ src, at[1] ^ z, at[2] ^ x, at[3])) for at in every]
        return lax.ppermute(array, AXES, pairs)

    def to_owner(array, far):
        pairs = [
            (place(s, z, x, r), place(s, z, x, r ^ 1)) for s, z, x, r in every if (r == z // half) == far
        ]
        return lax.ppermute(array, AXES, pairs)

    def owner_src(array, far):
        pairs = [
            (place(s, z, x, r), place(s ^ 1, z, x, r)) for s, z, x, r in every if (r == z // half) != far
        ]
        return lax.ppermute(array, AXES, pairs)

    def shards(tokens, coefficients, gate_weights, up_weights):
        rows = tokens.shape[1]
        own_tp, own_row = lax.axis_index("tp"), lax.axis_index("row")
        width = gate_weights.shape[2]

        def times(blocks, scale, work):
            return products(blocks, scale, coefficients, gate_held, up_held, work)

        b0 = tokens[0]
        gate_held, up_held = resident(gate_weights, up_weights, 1)
        z3 = swap(b0, z=3)
        z1 = swap(b0, z=1)
        y0 = swap(b0, src=1)
        x0 = swap(b0, x=1)
        d0 = swap(after(x0, gate_held), src=1)
        z2 = swap(z3, z=1)
        y1 = swap(z1, src=1)
        x1 = swap(z1, x=1)
        d1 = swap(y1, x=1)
        y3 = swap(z3, src=1)
        x3 = swap(z3, x=1)
        d3 = swap(d0, z=3)
        near = times([y0, d0, y1, d1, b0, x0, z1, x1], [1] * 4 + [0] * 4, 1)
        near_core = to_owner(near, False)
        split = 4 * rows
        near_other = owner_src(near[:split] + near_core[:split], False)
        near_own, near_own_core = near[split:], near_core[split:]
        y2 = swap(z2, src=1)
        x2 = swap(z2, x=1)
        d2 = swap(d3, z=1)
        far = times([y2, d2, y3, d3, z2, x2, z3, x3], [1] * 4 + [0] * 4, 1)
        far_core = to_owner(far, True)
        far_sum = far[:split] + far_core[:split]
        far_other = owner_src(far_sum, True)
        far_own, far_own_core = far[split:], far_core[split:]
        keeps_near = own_row == (own_tp >> 1) // half
        return activated(
            (near_own, near_own_core, near_other, far_own, far_own_core, far_other),
            keeps_near,
            own_tp & 1,
            own_tp >> 1 & 1,
            rows,
            width,
        )

    return shards


def solution(mesh):
    fits = mesh.shape["src"] == 2 and mesh.shape["tp"] == 8 and mesh.shape["row"] == 2
    return jax.shard_map(
        paired(mesh) if fits else gathered,
        mesh=mesh,
        in_specs=(P("src", "tp", "row"), P(), P("src", "row", "tp"), P("src", "row", "tp")),
        out_specs=P("src", "row", "tp"),
        check_vma=False,
    )
```

```python
import jax
import jax.numpy as jnp
from jax import lax
from jax.experimental import pallas as pl
from jax.experimental.pallas import tpu as pltpu
from jax.sharding import PartitionSpec as P

AXES = ("src", "tp", "row")


def gathered(tokens, coefficients, gate_weights, up_weights):
    local_rows = tokens.shape[1]
    half_width = tokens.shape[2]
    candidates = coefficients.shape[0]
    sources = coefficients.shape[1]
    per_candidate = local_rows * lax.axis_size("tp")
    out_rows = per_candidate // lax.axis_size("row")
    own_source = lax.axis_index("src")
    picked = (jnp.arange(sources, dtype=jnp.int32) == own_source).astype(jnp.float32)
    own_factors = jnp.sum(coefficients * picked[None, :], axis=1)
    gate_local = gate_weights[0]
    up_local = up_weights[0]
    hidden_width = gate_local.shape[1]
    flat_tokens = tokens.reshape(local_rows, half_width)
    row_block = lax.all_gather(flat_tokens, ("src", "tp"), axis=0, tiled=True)
    owner_ids = jnp.arange(row_block.shape[0], dtype=jnp.int32) // per_candidate
    one_hot = (owner_ids[:, None] == jnp.arange(candidates, dtype=jnp.int32)[None, :]).astype(
        jnp.float32
    )
    factor = jnp.sum(one_hot * own_factors[None, :], axis=1)[:, None]
    gate_part = jnp.dot(row_block, gate_local, preferred_element_type=jnp.float32)
    up_part = jnp.dot(row_block, up_local, preferred_element_type=jnp.float32)
    collected = jnp.concatenate((gate_part, up_part), axis=1) * factor
    summed = lax.psum_scatter(collected, ("src", "row"), scatter_dimension=0, tiled=True)
    hidden = (jax.nn.silu(summed[:, :hidden_width]) * summed[:, hidden_width:]).astype(jnp.bfloat16)
    return hidden.reshape(1, out_rows, hidden_width)


def after(array, *others):
    return lax.optimization_barrier((array,) + others)[0]


def keeps_near(half):
    return lax.axis_index("row") == (lax.axis_index("tp") >> 1) // half


def products(other, own, coefficients, weights, work, half, near=None):
    blocks = other + own
    count = len(blocks)
    rows, depth = blocks[0].shape
    width = weights[0].shape[2]
    span = len(other) * rows
    extra = 0 if near is None else 2

    def kernel(*refs):
        table, block_refs = refs[0], refs[1 : count + 1]
        gate, up = refs[count + 1 : count + 3]
        near_refs = refs[count + 3 : count + 3 + extra]
        outs = refs[count + 3 + extra :]
        source = lax.axis_index("src")
        lhs = jnp.concatenate([ref[...] for ref in block_refs], axis=0)
        factors = (table[1 - source, source], table[source, source])

        def store(targets):
            for start, held in ((0, gate), (width, up)):
                part = jnp.dot(lhs, held[0], preferred_element_type=jnp.float32)
                for i in range(2):
                    targets[i][:, start : start + width] = part[i * span : (i + 1) * span] * factors[i]

        if near is None:
            store(outs)
        else:
            sent, kept = outs[:2], outs[2:]
            mine = keeps_near(half)

            @pl.when(mine)
            def _():
                store(sent)
                for i in range(2):
                    kept[i][...] = near_refs[i][...]

            @pl.when(jnp.logical_not(mine))
            def _():
                store(kept)
                for i in range(2):
                    sent[i][...] = near_refs[i][...]

    whole = pl.BlockSpec(memory_space=pltpu.VMEM)
    result = jax.ShapeDtypeStruct((span, 2 * width), jnp.float32)
    return pl.pallas_call(
        kernel,
        out_shape=[result] * (2 + extra),
        in_specs=[pl.BlockSpec(memory_space=pltpu.SMEM)] + [whole] * (count + 2 + extra),
        out_specs=[whole] * (2 + extra),
        compiler_params=pltpu.CompilerParams(vmem_limit_bytes=24 * 2**20),
        cost_estimate=pl.CostEstimate(
            flops=work * 4 * count * rows * depth * width,
            bytes_accessed=4 * depth * width + 2 * count * rows * depth,
            transcendentals=0,
        ),
    )(coefficients, *blocks, *weights, *(near or ()))


def resident(gate_weights, up_weights, work):
    def kernel(gate, up, gate_out, up_out, sems):
        copies = [
            pltpu.make_async_copy(gate, gate_out, sems.at[0]),
            pltpu.make_async_copy(up, up_out, sems.at[1]),
        ]
        for copy in copies:
            copy.start()
        for copy in copies:
            copy.wait()

    size = gate_weights.size + up_weights.size
    return pl.pallas_call(
        kernel,
        out_shape=[pltpu.VMEM(w.shape, w.dtype) for w in (gate_weights, up_weights)],
        in_specs=[pl.BlockSpec(memory_space=pltpu.HBM)] * 2,
        out_specs=[pl.BlockSpec(memory_space=pltpu.VMEM)] * 2,
        scratch_shapes=[pltpu.SemaphoreType.DMA((2,))],
        compiler_params=pltpu.CompilerParams(vmem_limit_bytes=48 * 2**20),
        cost_estimate=pl.CostEstimate(
            flops=work * size, bytes_accessed=4 * size, transcendentals=0
        ),
    )(gate_weights, up_weights)


def activated(parts, rows):
    width = parts[0].shape[1] // 2

    def kernel(*refs):
        out = refs[-1]
        tp = lax.axis_index("tp")
        for i in range(4):
            span = slice(i * rows, (i + 1) * rows)
            total = refs[0][span, :] + refs[1][span, :] + refs[2][span, :]
            gate, up = total[:, :width], total[:, width:]
            value = (gate / (1 + jnp.exp(-gate)) * up).astype(jnp.bfloat16)
            at = i ^ (tp & 3)
            out[0, pl.ds(pl.multiple_of(at * rows, rows), rows), :] = value

    whole = pl.BlockSpec(memory_space=pltpu.VMEM)
    return pl.pallas_call(
        kernel,
        out_shape=jax.ShapeDtypeStruct((1, 4 * rows, width), jnp.bfloat16),
        in_specs=[whole] * 3,
        out_specs=whole,
        compiler_params=pltpu.CompilerParams(vmem_limit_bytes=24 * 2**20),
    )(*parts)


def paired(mesh):
    tp = mesh.shape["tp"]
    levels = tp // 2
    half = levels // 2

    def place(src, z, x, row):
        return (src * tp + z * 2 + x) * 2 + row

    every = [(s, z, x, r) for s in range(2) for z in range(levels) for x in range(2) for r in range(2)]

    def swap(array, src=0, z=0, x=0, row=0):
        pairs = [(place(*at), place(at[0] ^ src, at[1] ^ z, at[2] ^ x, at[3] ^ row)) for at in every]
        return lax.ppermute(array, AXES, pairs)

    def shards(tokens, coefficients, gate_weights, up_weights):
        rows = tokens.shape[1]
        b0 = tokens[0]
        held = resident(gate_weights, up_weights, 1)
        z3 = swap(b0, z=3)
        z1 = swap(b0, z=1)
        y0 = swap(b0, src=1)
        x0 = swap(b0, x=1)
        d0 = swap(after(x0, y0, held[0]), src=1)
        z2 = swap(z3, z=1)
        y1 = swap(z1, src=1)
        x1 = swap(z1, x=1)
        d1 = swap(after(y1, x1), x=1)
        y3 = swap(z3, src=1)
        x3 = swap(z3, x=1)
        d3 = swap(d0, z=3)
        near = products([y0, d0, y1, d1], [b0, x0, z1, x1], coefficients, held, 1, half)
        y2 = swap(z2, src=1)
        x2 = swap(z2, x=1)
        d2 = swap(d3, z=1)
        sent, sent_own, kept, kept_own = products(
            [y2, d2, y3, d3], [z2, x2, z3, x3], coefficients, held, 1, half, near
        )
        other = kept + swap(sent, row=1)
        core_own = swap(sent_own, row=1)
        from_other = swap(other, src=1)
        return activated((kept_own, core_own, from_other), rows)

    return shards


def solution(mesh):
    fits = mesh.shape["src"] == 2 and mesh.shape["tp"] == 8 and mesh.shape["row"] == 2
    return jax.shard_map(
        paired(mesh) if fits else gathered,
        mesh=mesh,
        in_specs=(P("src", "tp", "row"), P(), P("src", "row", "tp"), P("src", "row", "tp")),
        out_specs=P("src", "row", "tp"),
        check_vma=False,
    )
```

```python
import jax
import jax.numpy as jnp
from jax import lax
from jax.experimental import pallas as pl
from jax.experimental.pallas import tpu as pltpu
from jax.sharding import PartitionSpec as P

AXES = ("src", "tp", "row")


def gathered(tokens, coefficients, gate_weights, up_weights):
    local_rows = tokens.shape[1]
    half_width = tokens.shape[2]
    candidates = coefficients.shape[0]
    sources = coefficients.shape[1]
    per_candidate = local_rows * lax.axis_size("tp")
    out_rows = per_candidate // lax.axis_size("row")
    own_source = lax.axis_index("src")
    picked = (jnp.arange(sources, dtype=jnp.int32) == own_source).astype(jnp.float32)
    own_factors = jnp.sum(coefficients * picked[None, :], axis=1)
    gate_local = gate_weights[0]
    up_local = up_weights[0]
    hidden_width = gate_local.shape[1]
    flat_tokens = tokens.reshape(local_rows, half_width)
    row_block = lax.all_gather(flat_tokens, ("src", "tp"), axis=0, tiled=True)
    owner_ids = jnp.arange(row_block.shape[0], dtype=jnp.int32) // per_candidate
    one_hot = (owner_ids[:, None] == jnp.arange(candidates, dtype=jnp.int32)[None, :]).astype(
        jnp.float32
    )
    factor = jnp.sum(one_hot * own_factors[None, :], axis=1)[:, None]
    gate_part = jnp.dot(row_block, gate_local, preferred_element_type=jnp.float32)
    up_part = jnp.dot(row_block, up_local, preferred_element_type=jnp.float32)
    collected = jnp.concatenate((gate_part, up_part), axis=1) * factor
    summed = lax.psum_scatter(collected, ("src", "row"), scatter_dimension=0, tiled=True)
    hidden = (jax.nn.silu(summed[:, :hidden_width]) * summed[:, hidden_width:]).astype(jnp.bfloat16)
    return hidden.reshape(1, out_rows, hidden_width)


def after(array, *others):
    return lax.optimization_barrier((array,) + others)[0]


def keeps_near(half):
    return lax.axis_index("row") == (lax.axis_index("tp") >> 1) // half


def products(other, own, coefficients, weights, work, half, near=None):
    blocks = other + own
    count = len(blocks)
    rows, depth = blocks[0].shape
    width = weights[0].shape[2]
    span = len(other) * rows
    extra = 0 if near is None else 2

    def kernel(*refs):
        table, block_refs = refs[0], refs[1 : count + 1]
        gate, up = refs[count + 1 : count + 3]
        near_refs = refs[count + 3 : count + 3 + extra]
        outs = refs[count + 3 + extra :]
        source = lax.axis_index("src")
        lhs = jnp.concatenate([ref[...] for ref in block_refs], axis=0)
        factors = (table[1 - source, source], table[source, source])

        def store(targets):
            for start, held in ((0, gate), (width, up)):
                part = jnp.dot(lhs, held[0], preferred_element_type=jnp.float32)
                for i in range(2):
                    targets[i][:, start : start + width] = part[i * span : (i + 1) * span] * factors[i]

        if near is None:
            store(outs)
        else:
            sent, kept = outs[:2], outs[2:]
            mine = keeps_near(half)

            @pl.when(mine)
            def _():
                store(sent)
                for i in range(2):
                    kept[i][...] = near_refs[i][...]

            @pl.when(jnp.logical_not(mine))
            def _():
                store(kept)
                for i in range(2):
                    sent[i][...] = near_refs[i][...]

    whole = pl.BlockSpec(memory_space=pltpu.VMEM)
    result = jax.ShapeDtypeStruct((span, 2 * width), jnp.float32)
    return pl.pallas_call(
        kernel,
        out_shape=[result] * (2 + extra),
        in_specs=[pl.BlockSpec(memory_space=pltpu.SMEM)] + [whole] * (count + 2 + extra),
        out_specs=[whole] * (2 + extra),
        compiler_params=pltpu.CompilerParams(vmem_limit_bytes=24 * 2**20),
        cost_estimate=pl.CostEstimate(
            flops=work * 4 * count * rows * depth * width,
            bytes_accessed=4 * depth * width + 2 * count * rows * depth,
            transcendentals=0,
        ),
    )(coefficients, *blocks, *weights, *(near or ()))


def resident(gate_weights, up_weights, work):
    def kernel(gate, up, gate_out, up_out, sems):
        copies = [
            pltpu.make_async_copy(gate, gate_out, sems.at[0]),
            pltpu.make_async_copy(up, up_out, sems.at[1]),
        ]
        for copy in copies:
            copy.start()
        for copy in copies:
            copy.wait()

    size = gate_weights.size + up_weights.size
    return pl.pallas_call(
        kernel,
        out_shape=[pltpu.VMEM(w.shape, w.dtype) for w in (gate_weights, up_weights)],
        in_specs=[pl.BlockSpec(memory_space=pltpu.HBM)] * 2,
        out_specs=[pl.BlockSpec(memory_space=pltpu.VMEM)] * 2,
        scratch_shapes=[pltpu.SemaphoreType.DMA((2,))],
        compiler_params=pltpu.CompilerParams(vmem_limit_bytes=48 * 2**20),
        cost_estimate=pl.CostEstimate(
            flops=work * size, bytes_accessed=4 * size, transcendentals=0
        ),
    )(gate_weights, up_weights)


SEGMENTS = 7
STEPS = 4016
FIELD = 128
SHIFT = 125


def coded(kept, received):
    rows, width = kept.shape
    side = width // 2

    def kernel(kept_ref, received_ref, out):
        lane = lax.broadcasted_iota(jnp.int32, (rows, FIELD), 1)
        scales = []
        for start in (0, side):
            columns = slice(start, start + side)
            total = kept_ref[:, columns] + received_ref[:, columns]
            size = jnp.abs(total)
            top = jnp.maximum(jnp.max(size, axis=1, keepdims=True), 1e-30) * 1.01
            top = top.astype(jnp.bfloat16).astype(jnp.float32)
            scales.append(top)
            part = size * (1 / top)
            level = part * 2.0**SEGMENTS
            for k in range(1, SEGMENTS):
                level = jnp.minimum(level, part * 2.0 ** (SEGMENTS - k) + k)
            number = jnp.floor(level * STEPS + 0.5)
            power = jnp.floor(number * (1 / FIELD))
            fraction = (number - power * FIELD) * (1 / FIELD)
            value = jnp.exp2(power - SHIFT) * (1 + fraction)
            out[:, columns] = jnp.where(total < 0, -value, value).astype(jnp.bfloat16)
        out[:, width:] = jnp.where(lane < FIELD // 2, scales[0], scales[1]).astype(jnp.bfloat16)

    whole = pl.BlockSpec(memory_space=pltpu.VMEM)
    return pl.pallas_call(
        kernel,
        out_shape=jax.ShapeDtypeStruct((rows, width + FIELD), jnp.bfloat16),
        in_specs=[whole] * 2,
        out_specs=whole,
        compiler_params=pltpu.CompilerParams(vmem_limit_bytes=24 * 2**20),
    )(kept, received)


def decoded(values, scale):
    values = values.astype(jnp.float32)
    size = jnp.abs(values)
    power = jnp.floor(jnp.log2(size) + 0.001)
    fraction = jnp.floor((size * jnp.exp2(-power) - 1) * FIELD + 0.5)
    level = ((power + SHIFT) * FIELD + fraction) * (1 / STEPS)
    part = level * 2.0**-SEGMENTS
    for k in range(1, SEGMENTS):
        part = jnp.maximum(part, (level - k) * 2.0 ** (k - SEGMENTS))
    return jnp.where(values < 0, -part, part) * scale


def activated(kept, received, code, rows):
    width = kept.shape[1] // 2

    def kernel(kept_ref, received_ref, code_ref, out):
        tp = lax.axis_index("tp")
        for i in range(4):
            span = slice(i * rows, (i + 1) * rows)
            total = []
            for j in range(2):
                columns = slice(j * width, (j + 1) * width)
                at = 2 * width + j * (FIELD // 2)
                scale = code_ref[span, at : at + 1].astype(jnp.float32)
                own = kept_ref[span, columns] + received_ref[span, columns]
                total.append(own + decoded(code_ref[span, columns], scale))
            gate, up = total
            value = (gate / (1 + jnp.exp(-gate)) * up).astype(jnp.bfloat16)
            at = i ^ (tp & 3)
            out[0, pl.ds(pl.multiple_of(at * rows, rows), rows), :] = value

    whole = pl.BlockSpec(memory_space=pltpu.VMEM)
    return pl.pallas_call(
        kernel,
        out_shape=jax.ShapeDtypeStruct((1, 4 * rows, width), jnp.bfloat16),
        in_specs=[whole] * 3,
        out_specs=whole,
        compiler_params=pltpu.CompilerParams(vmem_limit_bytes=24 * 2**20),
    )(kept, received, code)


def paired(mesh):
    tp = mesh.shape["tp"]
    levels = tp // 2
    half = levels // 2

    def place(src, z, x, row):
        return (src * tp + z * 2 + x) * 2 + row

    every = [(s, z, x, r) for s in range(2) for z in range(levels) for x in range(2) for r in range(2)]

    def swap(array, src=0, z=0, x=0, row=0):
        pairs = [(place(*at), place(at[0] ^ src, at[1] ^ z, at[2] ^ x, at[3] ^ row)) for at in every]
        return lax.ppermute(array, AXES, pairs)

    def shards(tokens, coefficients, gate_weights, up_weights):
        rows = tokens.shape[1]
        b0 = tokens[0]
        held = resident(gate_weights, up_weights, 1)
        z3 = swap(b0, z=3)
        z1 = swap(b0, z=1)
        y0 = swap(b0, src=1)
        x0 = swap(b0, x=1)
        d0 = swap(after(x0, y0, held[0]), src=1)
        z2 = swap(z3, z=1)
        y1 = swap(z1, src=1)
        x1 = swap(z1, x=1)
        d1 = swap(after(y1, y1), x=1)
        y3 = swap(z3, src=1)
        x3 = swap(z3, x=1)
        d3 = swap(d0, z=3)
        near = products([y0, d0, y1, d1], [b0, x0, z1, x1], coefficients, held, 1, half)
        y2 = swap(z2, src=1)
        x2 = swap(z2, x=1)
        d2 = swap(d3, z=1)
        sent, sent_own, kept, kept_own = products(
            [y2, d2, y3, d3], [z2, x2, z3, x3], coefficients, held, 1, half, near
        )
        other = coded(kept, swap(sent, row=1))
        core_own = swap(sent_own, row=1)
        from_other = swap(other, src=1)
        return activated(kept_own, core_own, from_other, rows)

    return shards


def solution(mesh):
    fits = mesh.shape["src"] == 2 and mesh.shape["tp"] == 8 and mesh.shape["row"] == 2
    return jax.shard_map(
        paired(mesh) if fits else gathered,
        mesh=mesh,
        in_specs=(P("src", "tp", "row"), P(), P("src", "row", "tp"), P("src", "row", "tp")),
        out_specs=P("src", "row", "tp"),
        check_vma=False,
    )
```

```python
import jax
import jax.numpy as jnp
from jax import lax
from jax.experimental import pallas as pl
from jax.experimental.pallas import tpu as pltpu
from jax.sharding import PartitionSpec as P

AXES = ("src", "tp", "row")


def gathered(tokens, coefficients, gate_weights, up_weights):
    local_rows = tokens.shape[1]
    half_width = tokens.shape[2]
    candidates = coefficients.shape[0]
    sources = coefficients.shape[1]
    per_candidate = local_rows * lax.axis_size("tp")
    out_rows = per_candidate // lax.axis_size("row")
    own_source = lax.axis_index("src")
    picked = (jnp.arange(sources, dtype=jnp.int32) == own_source).astype(jnp.float32)
    own_factors = jnp.sum(coefficients * picked[None, :], axis=1)
    gate_local = gate_weights[0]
    up_local = up_weights[0]
    hidden_width = gate_local.shape[1]
    flat_tokens = tokens.reshape(local_rows, half_width)
    row_block = lax.all_gather(flat_tokens, ("src", "tp"), axis=0, tiled=True)
    owner_ids = jnp.arange(row_block.shape[0], dtype=jnp.int32) // per_candidate
    one_hot = (owner_ids[:, None] == jnp.arange(candidates, dtype=jnp.int32)[None, :]).astype(
        jnp.float32
    )
    factor = jnp.sum(one_hot * own_factors[None, :], axis=1)[:, None]
    gate_part = jnp.dot(row_block, gate_local, preferred_element_type=jnp.float32)
    up_part = jnp.dot(row_block, up_local, preferred_element_type=jnp.float32)
    collected = jnp.concatenate((gate_part, up_part), axis=1) * factor
    summed = lax.psum_scatter(collected, ("src", "row"), scatter_dimension=0, tiled=True)
    hidden = (jax.nn.silu(summed[:, :hidden_width]) * summed[:, hidden_width:]).astype(jnp.bfloat16)
    return hidden.reshape(1, out_rows, hidden_width)


def after(array, *others):
    return lax.optimization_barrier((array,) + others)[0]


def keeps_near(half):
    return lax.axis_index("row") == (lax.axis_index("tp") >> 1) // half


def products(blocks, own, coefficients, weights, work, half=None, near=None):
    count = len(blocks)
    rows, depth = blocks[0].shape
    width = weights[0].shape[2]
    earlier = () if near is None else (near,)
    split = half is not None and near is None
    span = count * rows // 2 if split else count * rows

    def kernel(*refs):
        table, block_refs = refs[0], refs[1 : count + 1]
        held = refs[count + 1 : count + 3]
        near_refs = refs[count + 3 : count + 3 + len(earlier)]
        outs = refs[count + 3 + len(earlier) :]
        source = lax.axis_index("src")
        factor = table[source, source] if own else table[1 - source, source]
        lhs = jnp.concatenate([ref[...] for ref in block_refs], axis=0)

        def store(*targets):
            for i in range(2):
                product = jnp.dot(lhs, held[i][0], preferred_element_type=jnp.float32)
                for j, target in enumerate(targets):
                    part = product[j * span : (j + 1) * span]
                    target[:, i * width : (i + 1) * width] = part * factor

        def fill(near_target, far_target):
            if split:
                store(near_target, far_target)
            else:
                store(far_target)
                near_target[...] = near_refs[0][...]

        if half is None:
            store(outs[0])
        else:
            mine = keeps_near(half)

            @pl.when(mine)
            def _():
                fill(outs[1], outs[0])

            @pl.when(jnp.logical_not(mine))
            def _():
                fill(outs[0], outs[1])

    whole = pl.BlockSpec(memory_space=pltpu.VMEM)
    results = 1 if half is None else 2
    out = pl.pallas_call(
        kernel,
        out_shape=[jax.ShapeDtypeStruct((span, 2 * width), jnp.float32)] * results,
        in_specs=[pl.BlockSpec(memory_space=pltpu.SMEM)] + [whole] * (count + 2 + len(earlier)),
        out_specs=[whole] * results,
        compiler_params=pltpu.CompilerParams(vmem_limit_bytes=24 * 2**20),
        cost_estimate=pl.CostEstimate(
            flops=work * 4 * count * rows * depth * width,
            bytes_accessed=4 * depth * width + 2 * count * rows * depth,
            transcendentals=0,
        ),
    )(coefficients, *blocks, *weights, *earlier)
    return out if half is not None else out[0]


def resident(gate_weights, up_weights, work):
    def kernel(gate, up, gate_out, up_out, sems):
        copies = [
            pltpu.make_async_copy(gate, gate_out, sems.at[0]),
            pltpu.make_async_copy(up, up_out, sems.at[1]),
        ]
        for copy in copies:
            copy.start()
        for copy in copies:
            copy.wait()

    size = gate_weights.size + up_weights.size
    return pl.pallas_call(
        kernel,
        out_shape=[pltpu.VMEM(w.shape, w.dtype) for w in (gate_weights, up_weights)],
        in_specs=[pl.BlockSpec(memory_space=pltpu.HBM)] * 2,
        out_specs=[pl.BlockSpec(memory_space=pltpu.VMEM)] * 2,
        scratch_shapes=[pltpu.SemaphoreType.DMA((2,))],
        compiler_params=pltpu.CompilerParams(vmem_limit_bytes=48 * 2**20),
        cost_estimate=pl.CostEstimate(
            flops=work * size, bytes_accessed=4 * size, transcendentals=0
        ),
    )(gate_weights, up_weights)


SEGMENTS = 7
STEPS = 4016
FIELD = 128
SHIFT = 125


def coded(kept, received):
    rows, width = kept.shape
    side = width // 2

    def kernel(kept_ref, received_ref, out):
        lane = lax.broadcasted_iota(jnp.int32, (rows, FIELD), 1)
        scales = []
        for start in (0, side):
            columns = slice(start, start + side)
            total = kept_ref[:, columns] + received_ref[:, columns]
            size = jnp.abs(total)
            top = jnp.maximum(jnp.max(size, axis=1, keepdims=True), 1e-30) * 1.01
            top = top.astype(jnp.bfloat16).astype(jnp.float32)
            scales.append(top)
            part = size * (1 / top)
            level = part * 2.0**SEGMENTS
            for k in range(1, SEGMENTS):
                level = jnp.minimum(level, part * 2.0 ** (SEGMENTS - k) + k)
            number = jnp.floor(level * STEPS + 0.5)
            power = jnp.floor(number * (1 / FIELD))
            fraction = (number - power * FIELD) * (1 / FIELD)
            value = jnp.exp2(power - SHIFT) * (1 + fraction)
            out[:, columns] = jnp.where(total < 0, -value, value).astype(jnp.bfloat16)
        out[:, width:] = jnp.where(lane < FIELD // 2, scales[0], scales[1]).astype(jnp.bfloat16)

    whole = pl.BlockSpec(memory_space=pltpu.VMEM)
    return pl.pallas_call(
        kernel,
        out_shape=jax.ShapeDtypeStruct((rows, width + FIELD), jnp.bfloat16),
        in_specs=[whole] * 2,
        out_specs=whole,
        compiler_params=pltpu.CompilerParams(vmem_limit_bytes=24 * 2**20),
    )(kept, received)


def decoded(values, work):
    rows, side = values.shape[0], (values.shape[1] - FIELD) // 2

    def kernel(values_ref, out):
        for j in range(2):
            columns = slice(j * side, (j + 1) * side)
            at = 2 * side + j * (FIELD // 2)
            scale = values_ref[:, at : at + 1].astype(jnp.float32)
            value = values_ref[:, columns].astype(jnp.float32)
            size = jnp.abs(value)
            power = jnp.floor(jnp.log2(size) + 0.001)
            fraction = jnp.floor((size * jnp.exp2(-power) - 1) * FIELD + 0.5)
            level = ((power + SHIFT) * FIELD + fraction) * (1 / STEPS)
            part = level * 2.0**-SEGMENTS
            for k in range(1, SEGMENTS):
                part = jnp.maximum(part, (level - k) * 2.0 ** (k - SEGMENTS))
            out[:, columns] = jnp.where(value < 0, -part, part) * scale

    whole = pl.BlockSpec(memory_space=pltpu.VMEM)
    return pl.pallas_call(
        kernel,
        out_shape=jax.ShapeDtypeStruct((rows, 2 * side), jnp.float32),
        in_specs=[whole],
        out_specs=whole,
        compiler_params=pltpu.CompilerParams(vmem_limit_bytes=24 * 2**20),
        cost_estimate=pl.CostEstimate(
            flops=work * 60 * rows * side, bytes_accessed=2 * values.size, transcendentals=0
        ),
    )(values)


def activated(parts, rows):
    width = parts[0].shape[1] // 2

    def kernel(*refs):
        out = refs[-1]
        tp = lax.axis_index("tp")
        for i in range(4):
            span = slice(i * rows, (i + 1) * rows)
            total = refs[0][span, :] + refs[1][span, :] + refs[2][span, :]
            gate, up = total[:, :width], total[:, width:]
            value = (gate / (1 + jnp.exp(-gate)) * up).astype(jnp.bfloat16)
            at = i ^ (tp & 3)
            out[0, pl.ds(pl.multiple_of(at * rows, rows), rows), :] = value

    whole = pl.BlockSpec(memory_space=pltpu.VMEM)
    return pl.pallas_call(
        kernel,
        out_shape=jax.ShapeDtypeStruct((1, 4 * rows, width), jnp.bfloat16),
        in_specs=[whole] * 3,
        out_specs=whole,
        compiler_params=pltpu.CompilerParams(vmem_limit_bytes=24 * 2**20),
    )(*parts)


def paired(mesh):
    tp = mesh.shape["tp"]
    levels = tp // 2
    half = levels // 2

    def place(src, z, x, row):
        return (src * tp + z * 2 + x) * 2 + row

    every = [(s, z, x, r) for s in range(2) for z in range(levels) for x in range(2) for r in range(2)]

    def swap(array, src=0, z=0, x=0, row=0):
        pairs = [(place(*at), place(at[0] ^ src, at[1] ^ z, at[2] ^ x, at[3] ^ row)) for at in every]
        return lax.ppermute(array, AXES, pairs)

    def shards(tokens, coefficients, gate_weights, up_weights):
        rows = tokens.shape[1]
        b0 = tokens[0]
        held = resident(gate_weights, up_weights, 1)
        z3 = swap(b0, z=3)
        z1 = swap(b0, z=1)
        y0 = swap(b0, src=1)
        x0 = swap(b0, x=1)
        d0 = swap(b0, src=1, x=1)
        y1 = swap(after(z1, y0, x0, held[0]), src=1)
        x1 = swap(z1, x=1)
        z2 = swap(z3, z=1)
        d1 = swap(y1, x=1)
        y3 = swap(z3, src=1)
        x3 = swap(z3, x=1)
        d3 = swap(d0, z=3)
        near = products([y0, d0, y1, d1], False, coefficients, held, 1)
        y2 = swap(z2, src=1)
        x2 = swap(z2, x=1)
        d2 = swap(d3, z=1)
        sent, kept = products([after(y2, x3), d2, y3, d3], False, coefficients, held, 1, half, near)
        other = coded(kept, swap(after(sent, x1), row=1))
        from_other = swap(other, src=1)
        sent_own, kept_own = products([after(b0, other), x0, z1, x1, z2, x2, z3, x3], True, coefficients, held, 1, half)
        core_own = swap(sent_own, row=1)
        theirs = decoded(from_other, 3000)
        return activated((kept_own, core_own, theirs), rows)

    return shards


def solution(mesh):
    fits = mesh.shape["src"] == 2 and mesh.shape["tp"] == 8 and mesh.shape["row"] == 2
    return jax.shard_map(
        paired(mesh) if fits else gathered,
        mesh=mesh,
        in_specs=(P("src", "tp", "row"), P(), P("src", "row", "tp"), P("src", "row", "tp")),
        out_specs=P("src", "row", "tp"),
        check_vma=False,
    )
```

```python
import jax
import jax.numpy as jnp
from jax import lax
from jax.experimental import pallas as pl
from jax.experimental.pallas import tpu as pltpu
from jax.sharding import PartitionSpec as P

AXES = ("src", "tp", "row")


def gathered(tokens, coefficients, gate_weights, up_weights):
    local_rows = tokens.shape[1]
    half_width = tokens.shape[2]
    candidates = coefficients.shape[0]
    sources = coefficients.shape[1]
    per_candidate = local_rows * lax.axis_size("tp")
    out_rows = per_candidate // lax.axis_size("row")
    own_source = lax.axis_index("src")
    picked = (jnp.arange(sources, dtype=jnp.int32) == own_source).astype(jnp.float32)
    own_factors = jnp.sum(coefficients * picked[None, :], axis=1)
    gate_local = gate_weights[0]
    up_local = up_weights[0]
    hidden_width = gate_local.shape[1]
    flat_tokens = tokens.reshape(local_rows, half_width)
    row_block = lax.all_gather(flat_tokens, ("src", "tp"), axis=0, tiled=True)
    owner_ids = jnp.arange(row_block.shape[0], dtype=jnp.int32) // per_candidate
    one_hot = (owner_ids[:, None] == jnp.arange(candidates, dtype=jnp.int32)[None, :]).astype(
        jnp.float32
    )
    factor = jnp.sum(one_hot * own_factors[None, :], axis=1)[:, None]
    gate_part = jnp.dot(row_block, gate_local, preferred_element_type=jnp.float32)
    up_part = jnp.dot(row_block, up_local, preferred_element_type=jnp.float32)
    collected = jnp.concatenate((gate_part, up_part), axis=1) * factor
    summed = lax.psum_scatter(collected, ("src", "row"), scatter_dimension=0, tiled=True)
    hidden = (jax.nn.silu(summed[:, :hidden_width]) * summed[:, hidden_width:]).astype(jnp.bfloat16)
    return hidden.reshape(1, out_rows, hidden_width)


def after(array, *others):
    return lax.optimization_barrier((array,) + others)[0]


def keeps_near(half):
    return lax.axis_index("row") == (lax.axis_index("tp") >> 1) // half


def products(blocks, own, coefficients, weights, work, half=None, near=None):
    count = len(blocks)
    rows, depth = blocks[0].shape
    width = weights[0].shape[2]
    earlier = () if near is None else (near,)
    split = half is not None and near is None
    span = count * rows // 2 if split else count * rows

    def kernel(*refs):
        table, block_refs = refs[0], refs[1 : count + 1]
        held = refs[count + 1 : count + 3]
        near_refs = refs[count + 3 : count + 3 + len(earlier)]
        outs = refs[count + 3 + len(earlier) :]
        source = lax.axis_index("src")
        factor = table[source, source] if own else table[1 - source, source]
        lhs = jnp.concatenate([ref[...] for ref in block_refs], axis=0)

        def store(*targets):
            for i in range(2):
                product = jnp.dot(lhs, held[i][0], preferred_element_type=jnp.float32)
                for j, target in enumerate(targets):
                    part = product[j * span : (j + 1) * span]
                    target[:, i * width : (i + 1) * width] = part * factor

        def fill(near_target, far_target):
            if split:
                store(near_target, far_target)
            else:
                store(far_target)
                near_target[...] = near_refs[0][...]

        if half is None:
            store(outs[0])
        else:
            mine = keeps_near(half)

            @pl.when(mine)
            def _():
                fill(outs[1], outs[0])

            @pl.when(jnp.logical_not(mine))
            def _():
                fill(outs[0], outs[1])

    whole = pl.BlockSpec(memory_space=pltpu.VMEM)
    results = 1 if half is None else 2
    out = pl.pallas_call(
        kernel,
        out_shape=[jax.ShapeDtypeStruct((span, 2 * width), jnp.float32)] * results,
        in_specs=[pl.BlockSpec(memory_space=pltpu.SMEM)] + [whole] * (count + 2 + len(earlier)),
        out_specs=[whole] * results,
        compiler_params=pltpu.CompilerParams(vmem_limit_bytes=24 * 2**20),
        cost_estimate=pl.CostEstimate(
            flops=work * 4 * count * rows * depth * width,
            bytes_accessed=4 * depth * width + 2 * count * rows * depth,
            transcendentals=0,
        ),
    )(coefficients, *blocks, *weights, *earlier)
    return out if half is not None else out[0]


def resident(gate_weights, up_weights, work):
    def kernel(gate, up, gate_out, up_out, sems):
        copies = [
            pltpu.make_async_copy(gate, gate_out, sems.at[0]),
            pltpu.make_async_copy(up, up_out, sems.at[1]),
        ]
        for copy in copies:
            copy.start()
        for copy in copies:
            copy.wait()

    size = gate_weights.size + up_weights.size
    return pl.pallas_call(
        kernel,
        out_shape=[pltpu.VMEM(w.shape, w.dtype) for w in (gate_weights, up_weights)],
        in_specs=[pl.BlockSpec(memory_space=pltpu.HBM)] * 2,
        out_specs=[pl.BlockSpec(memory_space=pltpu.VMEM)] * 2,
        scratch_shapes=[pltpu.SemaphoreType.DMA((2,))],
        compiler_params=pltpu.CompilerParams(vmem_limit_bytes=48 * 2**20),
        cost_estimate=pl.CostEstimate(
            flops=work * size, bytes_accessed=4 * size, transcendentals=0
        ),
    )(gate_weights, up_weights)


SEGMENTS = 7
STEPS = 4016
FIELD = 128
SHIFT = 125
TAIL = 16


def diagonal(side):
    shape = (side, side)
    return lax.broadcasted_iota(jnp.int32, shape, 0) == lax.broadcasted_iota(jnp.int32, shape, 1)


def coded(kept, received):
    rows, width = kept.shape
    side = width // 2

    def kernel(kept_ref, received_ref, out):
        scales = []
        for start in (0, side):
            columns = slice(start, start + side)
            total = kept_ref[:, columns] + received_ref[:, columns]
            size = jnp.abs(total)
            top = jnp.maximum(jnp.max(size, axis=1, keepdims=True), 1e-36) * 1.01
            top = top.astype(jnp.bfloat16).astype(jnp.float32)
            scales.append(jnp.sum(jnp.where(diagonal(rows), top, 0.0), axis=0, keepdims=True))
            part = size * (1 / top)
            level = part * 2.0**SEGMENTS
            for k in range(1, SEGMENTS):
                level = jnp.minimum(level, part * 2.0 ** (SEGMENTS - k) + k)
            number = jnp.floor(level * STEPS + 0.5)
            power = jnp.floor(number * (1 / FIELD))
            fraction = (number - power * FIELD) * (1 / FIELD)
            value = jnp.exp2(power - SHIFT) * (1 + fraction)
            value = jnp.where(total < 0, -value, value).astype(jnp.bfloat16)
            for at in range(0, side, rows):
                out[start + at : start + at + rows, :] = value[:, at : at + rows]
        row = lax.broadcasted_iota(jnp.int32, (TAIL, rows), 0)
        out[width:, :] = jnp.where(row == 0, scales[0], scales[1]).astype(jnp.bfloat16)

    whole = pl.BlockSpec(memory_space=pltpu.VMEM)
    return pl.pallas_call(
        kernel,
        out_shape=jax.ShapeDtypeStruct((width + TAIL, rows), jnp.bfloat16),
        in_specs=[whole] * 2,
        out_specs=whole,
        compiler_params=pltpu.CompilerParams(vmem_limit_bytes=24 * 2**20),
    )(kept, received)


def decoded(values, work):
    rows = values.shape[1]
    width = values.shape[0] - TAIL
    side = width // 2

    def kernel(values_ref, out):
        scales = values_ref[width:, :].astype(jnp.float32)
        for j in range(2):
            scale = jnp.sum(jnp.where(diagonal(rows), scales[j : j + 1, :], 0.0), axis=1, keepdims=True)
            for at in range(j * side, (j + 1) * side, rows):
                value = values_ref[at : at + rows, :].astype(jnp.float32)
                size = jnp.abs(value)
                power = jnp.floor(jnp.log2(size) + 0.001)
                fraction = jnp.floor((size * jnp.exp2(-power) - 1) * FIELD + 0.5)
                level = ((power + SHIFT) * FIELD + fraction) * (1 / STEPS)
                part = level * 2.0**-SEGMENTS
                for k in range(1, SEGMENTS):
                    part = jnp.maximum(part, (level - k) * 2.0 ** (k - SEGMENTS))
                out[:, at : at + rows] = jnp.where(value < 0, -part, part) * scale

    whole = pl.BlockSpec(memory_space=pltpu.VMEM)
    return pl.pallas_call(
        kernel,
        out_shape=jax.ShapeDtypeStruct((rows, width), jnp.float32),
        in_specs=[whole],
        out_specs=whole,
        compiler_params=pltpu.CompilerParams(vmem_limit_bytes=24 * 2**20),
        cost_estimate=pl.CostEstimate(
            flops=work * 30 * values.size, bytes_accessed=2 * values.size, transcendentals=0
        ),
    )(values)


def activated(parts, rows):
    width = parts[0].shape[1] // 2

    def kernel(*refs):
        out = refs[-1]
        tp = lax.axis_index("tp")
        for i in range(4):
            span = slice(i * rows, (i + 1) * rows)
            total = refs[0][span, :] + refs[1][span, :] + refs[2][span, :]
            gate, up = total[:, :width], total[:, width:]
            value = (gate / (1 + jnp.exp(-gate)) * up).astype(jnp.bfloat16)
            at = i ^ (tp & 3)
            out[0, pl.ds(pl.multiple_of(at * rows, rows), rows), :] = value

    whole = pl.BlockSpec(memory_space=pltpu.VMEM)
    return pl.pallas_call(
        kernel,
        out_shape=jax.ShapeDtypeStruct((1, 4 * rows, width), jnp.bfloat16),
        in_specs=[whole] * 3,
        out_specs=whole,
        compiler_params=pltpu.CompilerParams(vmem_limit_bytes=24 * 2**20),
    )(*parts)


def paired(mesh):
    tp = mesh.shape["tp"]
    levels = tp // 2
    half = levels // 2

    def place(src, z, x, row):
        return (src * tp + z * 2 + x) * 2 + row

    every = [(s, z, x, r) for s in range(2) for z in range(levels) for x in range(2) for r in range(2)]

    def swap(array, src=0, z=0, x=0, row=0):
        pairs = [(place(*at), place(at[0] ^ src, at[1] ^ z, at[2] ^ x, at[3] ^ row)) for at in every]
        return lax.ppermute(array, AXES, pairs)

    def shards(tokens, coefficients, gate_weights, up_weights):
        rows = tokens.shape[1]
        b0 = tokens[0]
        held = resident(gate_weights, up_weights, 1)
        z3 = swap(b0, z=3)
        z1 = swap(b0, z=1)
        y0 = swap(b0, src=1)
        x0 = swap(b0, x=1)
        d0 = swap(b0, src=1, x=1)
        y1 = swap(after(z1, y0, x0, held[0]), src=1)
        x1 = swap(z1, x=1)
        z2 = swap(z3, z=1)
        d1 = swap(y1, x=1)
        y3 = swap(z3, src=1)
        x3 = swap(z3, x=1)
        d3 = swap(d0, z=3)
        near = products([y0, d0, y1, d1], False, coefficients, held, 1)
        y2 = swap(z2, src=1)
        x2 = swap(z2, x=1)
        d2 = swap(d3, z=1)
        sent, kept = products([after(y2, x3), d2, y3, d3], False, coefficients, held, 1, half, near)
        other = coded(kept, swap(after(sent, x1), row=1))
        from_other = swap(other, src=1)
        near_own = products([b0, x0, z1, x1], True, coefficients, held, 1)
        sent_own, kept_own = products([z2, x2, z3, x3], True, coefficients, held, 1, half, near_own)
        core_own = swap(sent_own, row=1)
        theirs = decoded(from_other, 3000)
        return activated((kept_own, core_own, theirs), rows)

    return shards


def solution(mesh):
    fits = mesh.shape["src"] == 2 and mesh.shape["tp"] == 8 and mesh.shape["row"] == 2
    return jax.shard_map(
        paired(mesh) if fits else gathered,
        mesh=mesh,
        in_specs=(P("src", "tp", "row"), P(), P("src", "row", "tp"), P("src", "row", "tp")),
        out_specs=P("src", "row", "tp"),
        check_vma=False,
    )
```

```python
import jax
import jax.numpy as jnp
from jax import lax
from jax.experimental import pallas as pl
from jax.experimental.pallas import tpu as pltpu
from jax.sharding import PartitionSpec as P

AXES = ("src", "tp", "row")


def gathered(tokens, coefficients, gate_weights, up_weights):
    local_rows = tokens.shape[1]
    half_width = tokens.shape[2]
    candidates = coefficients.shape[0]
    sources = coefficients.shape[1]
    per_candidate = local_rows * lax.axis_size("tp")
    out_rows = per_candidate // lax.axis_size("row")
    own_source = lax.axis_index("src")
    picked = (jnp.arange(sources, dtype=jnp.int32) == own_source).astype(jnp.float32)
    own_factors = jnp.sum(coefficients * picked[None, :], axis=1)
    gate_local = gate_weights[0]
    up_local = up_weights[0]
    hidden_width = gate_local.shape[1]
    flat_tokens = tokens.reshape(local_rows, half_width)
    row_block = lax.all_gather(flat_tokens, ("src", "tp"), axis=0, tiled=True)
    owner_ids = jnp.arange(row_block.shape[0], dtype=jnp.int32) // per_candidate
    one_hot = (owner_ids[:, None] == jnp.arange(candidates, dtype=jnp.int32)[None, :]).astype(
        jnp.float32
    )
    factor = jnp.sum(one_hot * own_factors[None, :], axis=1)[:, None]
    gate_part = jnp.dot(row_block, gate_local, preferred_element_type=jnp.float32)
    up_part = jnp.dot(row_block, up_local, preferred_element_type=jnp.float32)
    collected = jnp.concatenate((gate_part, up_part), axis=1) * factor
    summed = lax.psum_scatter(collected, ("src", "row"), scatter_dimension=0, tiled=True)
    hidden = (jax.nn.silu(summed[:, :hidden_width]) * summed[:, hidden_width:]).astype(jnp.bfloat16)
    return hidden.reshape(1, out_rows, hidden_width)


def after(array, *others):
    return lax.optimization_barrier((array,) + others)[0]


def keeps_near(half):
    return lax.axis_index("row") == (lax.axis_index("tp") >> 1) // half


def products(blocks, own, coefficients, weights, work, half=None, near=None):
    count = len(blocks)
    rows, depth = blocks[0].shape
    width = weights[0].shape[2]
    earlier = () if near is None else (near,)
    split = half is not None and near is None
    span = count * rows // 2 if split else count * rows

    def kernel(*refs):
        table, block_refs = refs[0], refs[1 : count + 1]
        held = refs[count + 1 : count + 3]
        near_refs = refs[count + 3 : count + 3 + len(earlier)]
        outs = refs[count + 3 + len(earlier) :]
        source = lax.axis_index("src")
        factor = table[source, source] if own else table[1 - source, source]
        lhs = jnp.concatenate([ref[...] for ref in block_refs], axis=0)

        def store(*targets):
            for i in range(2):
                product = jnp.dot(lhs, held[i][0], preferred_element_type=jnp.float32)
                for j, target in enumerate(targets):
                    part = product[j * span : (j + 1) * span]
                    target[:, i * width : (i + 1) * width] = part * factor

        def fill(near_target, far_target):
            if split:
                store(near_target, far_target)
            else:
                store(far_target)
                near_target[...] = near_refs[0][...]

        if half is None:
            store(outs[0])
        else:
            mine = keeps_near(half)

            @pl.when(mine)
            def _():
                fill(outs[1], outs[0])

            @pl.when(jnp.logical_not(mine))
            def _():
                fill(outs[0], outs[1])

    whole = pl.BlockSpec(memory_space=pltpu.VMEM)
    results = 1 if half is None else 2
    out = pl.pallas_call(
        kernel,
        out_shape=[jax.ShapeDtypeStruct((span, 2 * width), jnp.float32)] * results,
        in_specs=[pl.BlockSpec(memory_space=pltpu.SMEM)] + [whole] * (count + 2 + len(earlier)),
        out_specs=[whole] * results,
        compiler_params=pltpu.CompilerParams(vmem_limit_bytes=24 * 2**20),
        cost_estimate=pl.CostEstimate(
            flops=work * 4 * count * rows * depth * width,
            bytes_accessed=4 * depth * width + 2 * count * rows * depth,
            transcendentals=0,
        ),
    )(coefficients, *blocks, *weights, *earlier)
    return out if half is not None else out[0]


def resident(gate_weights, up_weights, work):
    def kernel(gate, up, gate_out, up_out, sems):
        copies = [
            pltpu.make_async_copy(gate, gate_out, sems.at[0]),
            pltpu.make_async_copy(up, up_out, sems.at[1]),
        ]
        for copy in copies:
            copy.start()
        for copy in copies:
            copy.wait()

    size = gate_weights.size + up_weights.size
    return pl.pallas_call(
        kernel,
        out_shape=[pltpu.VMEM(w.shape, w.dtype) for w in (gate_weights, up_weights)],
        in_specs=[pl.BlockSpec(memory_space=pltpu.HBM)] * 2,
        out_specs=[pl.BlockSpec(memory_space=pltpu.VMEM)] * 2,
        scratch_shapes=[pltpu.SemaphoreType.DMA((2,))],
        compiler_params=pltpu.CompilerParams(vmem_limit_bytes=48 * 2**20),
        cost_estimate=pl.CostEstimate(
            flops=work * size, bytes_accessed=4 * size, transcendentals=0
        ),
    )(gate_weights, up_weights)


SEGMENTS = 7
STEPS = 4016
FIELD = 128
SHIFT = 125
TAIL = 16


def diagonal(side):
    shape = (side, side)
    return lax.broadcasted_iota(jnp.int32, shape, 0) == lax.broadcasted_iota(jnp.int32, shape, 1)


def coded(kept, received):
    rows, width = kept.shape
    side = width // 2

    def kernel(kept_ref, received_ref, out):
        scales = []
        for start in (0, side):
            columns = slice(start, start + side)
            total = kept_ref[:, columns] + received_ref[:, columns]
            size = jnp.abs(total)
            top = jnp.maximum(jnp.max(size, axis=1, keepdims=True), 1e-36) * 1.01
            top = top.astype(jnp.bfloat16).astype(jnp.float32)
            scales.append(jnp.sum(jnp.where(diagonal(rows), top, 0.0), axis=0, keepdims=True))
            part = size * (1 / top)
            level = part * 2.0**SEGMENTS
            for k in range(1, SEGMENTS):
                level = jnp.minimum(level, part * 2.0 ** (SEGMENTS - k) + k)
            number = jnp.floor(level * STEPS + 0.5)
            power = jnp.floor(number * (1 / FIELD))
            fraction = (number - power * FIELD) * (1 / FIELD)
            value = jnp.exp2(power - SHIFT) * (1 + fraction)
            value = jnp.where(total < 0, -value, value).astype(jnp.bfloat16)
            for at in range(0, side, rows):
                out[start + at : start + at + rows, :] = value[:, at : at + rows]
        row = lax.broadcasted_iota(jnp.int32, (TAIL, rows), 0)
        out[width:, :] = jnp.where(row == 0, scales[0], scales[1]).astype(jnp.bfloat16)

    whole = pl.BlockSpec(memory_space=pltpu.VMEM)
    return pl.pallas_call(
        kernel,
        out_shape=jax.ShapeDtypeStruct((width + TAIL, rows), jnp.bfloat16),
        in_specs=[whole] * 2,
        out_specs=whole,
        compiler_params=pltpu.CompilerParams(vmem_limit_bytes=24 * 2**20),
    )(kept, received)


def decoded(values, work):
    rows = values.shape[1]
    width = values.shape[0] - TAIL
    side = width // 2

    def kernel(values_ref, out):
        scales = values_ref[width:, :].astype(jnp.float32)
        for j in range(2):
            scale = jnp.sum(jnp.where(diagonal(rows), scales[j : j + 1, :], 0.0), axis=1, keepdims=True)
            for at in range(j * side, (j + 1) * side, rows):
                value = values_ref[at : at + rows, :].astype(jnp.float32)
                size = jnp.abs(value)
                power = jnp.floor(jnp.log2(size) + 0.001)
                fraction = jnp.floor((size * jnp.exp2(-power) - 1) * FIELD + 0.5)
                level = ((power + SHIFT) * FIELD + fraction) * (1 / STEPS)
                part = level * 2.0**-SEGMENTS
                for k in range(1, SEGMENTS):
                    part = jnp.maximum(part, (level - k) * 2.0 ** (k - SEGMENTS))
                out[:, at : at + rows] = jnp.where(value < 0, -part, part) * scale

    whole = pl.BlockSpec(memory_space=pltpu.VMEM)
    return pl.pallas_call(
        kernel,
        out_shape=jax.ShapeDtypeStruct((rows, width), jnp.float32),
        in_specs=[whole],
        out_specs=whole,
        compiler_params=pltpu.CompilerParams(vmem_limit_bytes=24 * 2**20),
        cost_estimate=pl.CostEstimate(
            flops=work * 30 * values.size, bytes_accessed=2 * values.size, transcendentals=0
        ),
    )(values)


def activated(parts, rows):
    width = parts[0].shape[1] // 2

    def kernel(*refs):
        out = refs[-1]
        tp = lax.axis_index("tp")
        for i in range(4):
            span = slice(i * rows, (i + 1) * rows)
            total = refs[0][span, :] + refs[1][span, :] + refs[2][span, :]
            gate, up = total[:, :width], total[:, width:]
            value = (gate / (1 + jnp.exp(-gate)) * up).astype(jnp.bfloat16)
            at = i ^ (tp & 3)
            out[0, pl.ds(pl.multiple_of(at * rows, rows), rows), :] = value

    whole = pl.BlockSpec(memory_space=pltpu.VMEM)
    return pl.pallas_call(
        kernel,
        out_shape=jax.ShapeDtypeStruct((1, 4 * rows, width), jnp.bfloat16),
        in_specs=[whole] * 3,
        out_specs=whole,
        compiler_params=pltpu.CompilerParams(vmem_limit_bytes=24 * 2**20),
    )(*parts)


def paired(mesh):
    tp = mesh.shape["tp"]
    levels = tp // 2
    half = levels // 2

    def place(src, z, x, row):
        return (src * tp + z * 2 + x) * 2 + row

    every = [(s, z, x, r) for s in range(2) for z in range(levels) for x in range(2) for r in range(2)]

    def swap(array, src=0, z=0, x=0, row=0):
        pairs = [(place(*at), place(at[0] ^ src, at[1] ^ z, at[2] ^ x, at[3] ^ row)) for at in every]
        return lax.ppermute(array, AXES, pairs)

    def shards(tokens, coefficients, gate_weights, up_weights):
        rows = tokens.shape[1]
        b0 = tokens[0]
        held = resident(gate_weights, up_weights, 1)
        z3 = swap(b0, z=3)
        z1 = swap(b0, z=1)
        y0 = swap(b0, src=1)
        x0 = swap(b0, x=1)
        d0 = swap(b0, src=1, x=1)
        y1 = swap(after(z1, y0, x0), src=1)
        x1 = swap(z1, x=1)
        z2 = swap(after(z3, held[0]), z=1)
        d1 = swap(y1, x=1)
        y3 = swap(z3, src=1)
        x3 = swap(z3, x=1)
        d3 = swap(d0, z=3)
        near = products([y0, d0, y1, d1], False, coefficients, held, 1)
        y2 = swap(z2, src=1)
        x2 = swap(z2, x=1)
        d2 = swap(d3, z=1)
        sent, kept = products([after(y2, x3), d2, y3, d3], False, coefficients, held, 1, half, near)
        other = coded(kept, swap(after(sent, x1), row=1))
        from_other = swap(other, src=1)
        near_own = products([b0, x0, z1, x1], True, coefficients, held, 1)
        sent_own, kept_own = products([z2, x2, z3, x3], True, coefficients, held, 1, half, near_own)
        core_own = swap(sent_own, row=1)
        theirs = decoded(from_other, 3000)
        return activated((kept_own, core_own, theirs), rows)

    return shards


def solution(mesh):
    fits = mesh.shape["src"] == 2 and mesh.shape["tp"] == 8 and mesh.shape["row"] == 2
    return jax.shard_map(
        paired(mesh) if fits else gathered,
        mesh=mesh,
        in_specs=(P("src", "tp", "row"), P(), P("src", "row", "tp"), P("src", "row", "tp")),
        out_specs=P("src", "row", "tp"),
        check_vma=False,
    )
```

```python
import jax
import jax.numpy as jnp
from jax import lax
from jax.experimental import pallas as pl
from jax.experimental.pallas import tpu as pltpu
from jax.sharding import PartitionSpec as P

AXES = ("src", "tp", "row")


def gathered(tokens, coefficients, gate_weights, up_weights):
    local_rows = tokens.shape[1]
    half_width = tokens.shape[2]
    candidates = coefficients.shape[0]
    sources = coefficients.shape[1]
    per_candidate = local_rows * lax.axis_size("tp")
    out_rows = per_candidate // lax.axis_size("row")
    own_source = lax.axis_index("src")
    picked = (jnp.arange(sources, dtype=jnp.int32) == own_source).astype(jnp.float32)
    own_factors = jnp.sum(coefficients * picked[None, :], axis=1)
    gate_local = gate_weights[0]
    up_local = up_weights[0]
    hidden_width = gate_local.shape[1]
    flat_tokens = tokens.reshape(local_rows, half_width)
    row_block = lax.all_gather(flat_tokens, ("src", "tp"), axis=0, tiled=True)
    owner_ids = jnp.arange(row_block.shape[0], dtype=jnp.int32) // per_candidate
    one_hot = (owner_ids[:, None] == jnp.arange(candidates, dtype=jnp.int32)[None, :]).astype(
        jnp.float32
    )
    factor = jnp.sum(one_hot * own_factors[None, :], axis=1)[:, None]
    gate_part = jnp.dot(row_block, gate_local, preferred_element_type=jnp.float32)
    up_part = jnp.dot(row_block, up_local, preferred_element_type=jnp.float32)
    collected = jnp.concatenate((gate_part, up_part), axis=1) * factor
    summed = lax.psum_scatter(collected, ("src", "row"), scatter_dimension=0, tiled=True)
    hidden = (jax.nn.silu(summed[:, :hidden_width]) * summed[:, hidden_width:]).astype(jnp.bfloat16)
    return hidden.reshape(1, out_rows, hidden_width)


def after(array, *others):
    return lax.optimization_barrier((array,) + others)[0]


def keeps_near(half):
    return lax.axis_index("row") == (lax.axis_index("tp") >> 1) // half


def products(blocks, own, coefficients, weights, work, half=None, near=None):
    count = len(blocks)
    rows, depth = blocks[0].shape
    width = weights[0].shape[2]
    earlier = () if near is None else (near,)
    split = half is not None and near is None
    span = count * rows // 2 if split else count * rows

    def kernel(*refs):
        table, block_refs = refs[0], refs[1 : count + 1]
        held = refs[count + 1 : count + 3]
        near_refs = refs[count + 3 : count + 3 + len(earlier)]
        outs = refs[count + 3 + len(earlier) :]
        source = lax.axis_index("src")
        factor = table[source, source] if own else table[1 - source, source]
        lhs = jnp.concatenate([ref[...] for ref in block_refs], axis=0)

        def store(*targets):
            for i in range(2):
                product = jnp.dot(lhs, held[i][0], preferred_element_type=jnp.float32)
                for j, target in enumerate(targets):
                    part = product[j * span : (j + 1) * span]
                    target[:, i * width : (i + 1) * width] = part * factor

        def fill(near_target, far_target):
            if split:
                store(near_target, far_target)
            else:
                store(far_target)
                near_target[...] = near_refs[0][...]

        if half is None:
            store(outs[0])
        else:
            mine = keeps_near(half)

            @pl.when(mine)
            def _():
                fill(outs[1], outs[0])

            @pl.when(jnp.logical_not(mine))
            def _():
                fill(outs[0], outs[1])

    whole = pl.BlockSpec(memory_space=pltpu.VMEM)
    results = 1 if half is None else 2
    out = pl.pallas_call(
        kernel,
        out_shape=[jax.ShapeDtypeStruct((span, 2 * width), jnp.float32)] * results,
        in_specs=[pl.BlockSpec(memory_space=pltpu.SMEM)] + [whole] * (count + 2 + len(earlier)),
        out_specs=[whole] * results,
        compiler_params=pltpu.CompilerParams(vmem_limit_bytes=24 * 2**20),
        cost_estimate=pl.CostEstimate(
            flops=work * 4 * count * rows * depth * width,
            bytes_accessed=4 * depth * width + 2 * count * rows * depth,
            transcendentals=0,
        ),
    )(coefficients, *blocks, *weights, *earlier)
    return out if half is not None else out[0]


def resident(gate_weights, up_weights, work):
    parts = 4
    step = gate_weights.shape[1] // parts

    def kernel(gate, up, gate_out, up_out, sems):
        copies = []
        for i, (source, target) in enumerate(((gate, gate_out), (up, up_out))):
            for n in range(parts):
                at = pl.ds(n * step, step)
                copies.append(
                    pltpu.make_async_copy(source.at[0, at, :], target.at[0, at, :], sems.at[i, n])
                )
        for copy in copies:
            copy.start()
        for copy in copies:
            copy.wait()

    size = gate_weights.size + up_weights.size
    return pl.pallas_call(
        kernel,
        out_shape=[pltpu.VMEM(w.shape, w.dtype) for w in (gate_weights, up_weights)],
        in_specs=[pl.BlockSpec(memory_space=pltpu.HBM)] * 2,
        out_specs=[pl.BlockSpec(memory_space=pltpu.VMEM)] * 2,
        scratch_shapes=[pltpu.SemaphoreType.DMA((2, parts))],
        compiler_params=pltpu.CompilerParams(vmem_limit_bytes=48 * 2**20),
        cost_estimate=pl.CostEstimate(
            flops=work * size, bytes_accessed=4 * size, transcendentals=0
        ),
    )(gate_weights, up_weights)


SEGMENTS = 7
STEPS = 4016
FIELD = 128
SHIFT = 125
TAIL = 16


def diagonal(side):
    shape = (side, side)
    return lax.broadcasted_iota(jnp.int32, shape, 0) == lax.broadcasted_iota(jnp.int32, shape, 1)


def coded(kept, received):
    rows, width = kept.shape
    side = width // 2

    def kernel(kept_ref, received_ref, out):
        scales = []
        for start in (0, side):
            columns = slice(start, start + side)
            total = kept_ref[:, columns] + received_ref[:, columns]
            size = jnp.abs(total)
            top = jnp.maximum(jnp.max(size, axis=1, keepdims=True), 1e-36) * 1.01
            top = top.astype(jnp.bfloat16).astype(jnp.float32)
            scales.append(jnp.sum(jnp.where(diagonal(rows), top, 0.0), axis=0, keepdims=True))
            part = size * (1 / top)
            level = part * 2.0**SEGMENTS
            for k in range(1, SEGMENTS):
                level = jnp.minimum(level, part * 2.0 ** (SEGMENTS - k) + k)
            number = jnp.floor(level * STEPS + 0.5)
            power = jnp.floor(number * (1 / FIELD))
            fraction = (number - power * FIELD) * (1 / FIELD)
            value = jnp.exp2(power - SHIFT) * (1 + fraction)
            value = jnp.where(total < 0, -value, value).astype(jnp.bfloat16)
            for at in range(0, side, rows):
                out[start + at : start + at + rows, :] = value[:, at : at + rows]
        row = lax.broadcasted_iota(jnp.int32, (TAIL, rows), 0)
        out[width:, :] = jnp.where(row == 0, scales[0], scales[1]).astype(jnp.bfloat16)

    whole = pl.BlockSpec(memory_space=pltpu.VMEM)
    return pl.pallas_call(
        kernel,
        out_shape=jax.ShapeDtypeStruct((width + TAIL, rows), jnp.bfloat16),
        in_specs=[whole] * 2,
        out_specs=whole,
        compiler_params=pltpu.CompilerParams(vmem_limit_bytes=24 * 2**20),
    )(kept, received)


def decoded(values, work):
    rows = values.shape[1]
    width = values.shape[0] - TAIL
    side = width // 2

    def kernel(values_ref, out):
        scales = values_ref[width:, :].astype(jnp.float32)
        for j in range(2):
            scale = jnp.sum(jnp.where(diagonal(rows), scales[j : j + 1, :], 0.0), axis=1, keepdims=True)
            for at in range(j * side, (j + 1) * side, rows):
                value = values_ref[at : at + rows, :].astype(jnp.float32)
                size = jnp.abs(value)
                power = jnp.floor(jnp.log2(size) + 0.001)
                fraction = jnp.floor((size * jnp.exp2(-power) - 1) * FIELD + 0.5)
                level = ((power + SHIFT) * FIELD + fraction) * (1 / STEPS)
                part = level * 2.0**-SEGMENTS
                for k in range(1, SEGMENTS):
                    part = jnp.maximum(part, (level - k) * 2.0 ** (k - SEGMENTS))
                out[:, at : at + rows] = jnp.where(value < 0, -part, part) * scale

    whole = pl.BlockSpec(memory_space=pltpu.VMEM)
    return pl.pallas_call(
        kernel,
        out_shape=jax.ShapeDtypeStruct((rows, width), jnp.float32),
        in_specs=[whole],
        out_specs=whole,
        compiler_params=pltpu.CompilerParams(vmem_limit_bytes=24 * 2**20),
        cost_estimate=pl.CostEstimate(
            flops=work * 30 * values.size, bytes_accessed=2 * values.size, transcendentals=0
        ),
    )(values)


def activated(parts, rows):
    width = parts[0].shape[1] // 2

    def kernel(*refs):
        out = refs[-1]
        tp = lax.axis_index("tp")
        for i in range(4):
            span = slice(i * rows, (i + 1) * rows)
            total = refs[0][span, :] + refs[1][span, :] + refs[2][span, :]
            gate, up = total[:, :width], total[:, width:]
            value = (gate / (1 + jnp.exp(-gate)) * up).astype(jnp.bfloat16)
            at = i ^ (tp & 3)
            out[0, pl.ds(pl.multiple_of(at * rows, rows), rows), :] = value

    whole = pl.BlockSpec(memory_space=pltpu.VMEM)
    return pl.pallas_call(
        kernel,
        out_shape=jax.ShapeDtypeStruct((1, 4 * rows, width), jnp.bfloat16),
        in_specs=[whole] * 3,
        out_specs=whole,
        compiler_params=pltpu.CompilerParams(vmem_limit_bytes=24 * 2**20),
    )(*parts)


def paired(mesh):
    tp = mesh.shape["tp"]
    levels = tp // 2
    half = levels // 2

    def place(src, z, x, row):
        return (src * tp + z * 2 + x) * 2 + row

    every = [(s, z, x, r) for s in range(2) for z in range(levels) for x in range(2) for r in range(2)]

    def swap(array, src=0, z=0, x=0, row=0):
        pairs = [(place(*at), place(at[0] ^ src, at[1] ^ z, at[2] ^ x, at[3] ^ row)) for at in every]
        return lax.ppermute(array, AXES, pairs)

    def shards(tokens, coefficients, gate_weights, up_weights):
        rows = tokens.shape[1]
        b0 = tokens[0]
        held = resident(gate_weights, up_weights, 1)
        z3 = swap(b0, z=3)
        z1 = swap(b0, z=1)
        y0 = swap(b0, src=1)
        x0 = swap(b0, x=1)
        d0 = swap(b0, src=1, x=1)
        y1 = swap(after(z1, y0, x0, held[0]), src=1)
        x1 = swap(z1, x=1)
        z2 = swap(z3, z=1)
        d1 = swap(y1, x=1)
        y3 = swap(z3, src=1)
        x3 = swap(z3, x=1)
        d3 = swap(d0, z=3)
        near = products([y0, d0, y1, d1], False, coefficients, held, 1)
        y2 = swap(z2, src=1)
        x2 = swap(z2, x=1)
        d2 = swap(d3, z=1)
        sent, kept = products([after(y2, x3), d2, y3, d3], False, coefficients, held, 1, half, near)
        other = coded(kept, swap(after(sent, x1), row=1))
        from_other = swap(other, src=1)
        near_own = products([b0, x0, z1, x1], True, coefficients, held, 1)
        sent_own, kept_own = products([z2, x2, z3, x3], True, coefficients, held, 1, half, near_own)
        core_own = swap(sent_own, row=1)
        theirs = decoded(from_other, 3000)
        return activated((kept_own, core_own, theirs), rows)

    return shards


def solution(mesh):
    fits = mesh.shape["src"] == 2 and mesh.shape["tp"] == 8 and mesh.shape["row"] == 2
    return jax.shard_map(
        paired(mesh) if fits else gathered,
        mesh=mesh,
        in_specs=(P("src", "tp", "row"), P(), P("src", "row", "tp"), P("src", "row", "tp")),
        out_specs=P("src", "row", "tp"),
        check_vma=False,
    )
```
